32 devices in a mesh: leaf: 4 (over z), grid: 8 (over y, x, core).
Axes of the slice: x: 2, y: 2, z: 4, core: 2. Of those that a mesh axis runs over, the one named last changes fastest.
Arguments:
- root_inverse: float32 [4096, 4096], P('grid', 'leaf'), may hold values from -1 to 12, as said below
- middle_inverse: float32 [2048, 4096], P('grid', 'leaf'), may hold values from -1 to 12, as said below
- middle_panel: float32 [4096, 4096], P('grid', 'leaf'), may hold values from -0.1875 to 0.1875
- lower_root: float32 [4096, 8192], P('grid', 'leaf'), may hold values from -0.1875 to 0.1875
- lower_middle: float32 [2048, 8192], P(None, 'leaf'), may hold values from -0.25 to 0.25
- block_pattern: int32 [4, 32], replicated, may hold values 0 or 1
- lower_diagonal: float32 [8192], P('leaf'), may hold values from 1.5 to 6
Outputs:
- middle_cross: float32 [4096, 4096], P('grid', 'leaf')
- middle_variance: float32 [4096], P('leaf')
- lower_cross: float32 [4096, 8192], P('grid', 'leaf')
- lower_parent: float32 [2048, 8192], P('grid', 'leaf')
- lower_variance: float32 [8192], P('leaf')
The draws below stay inside these ranges and needn't reach their ends.
Inputs may be any that keep to these rules, and one draw needn't show every extreme that they name: `root_inverse`: symmetric; its diagonal entries lie between 1.5 and 12. `middle_inverse`: each front's 2048 x 2048 block is symmetric; its diagonal entries lie between 1.5 and 12.
All inputs are finite; a program needn't handle non-finite values.
Results may differ from the reference program's by a relative error of at most 0.0001.
Values sent between devices are 32-bit elements; how exact they have to be, the bound alone decides.
No kernel may reach another device: no remote copies, remote signals or barrier semaphores. Data moves between devices by JAX's collectives and lax.ppermute only.
A program may use at most 192 MiB of HBM per device.

```python
import math
import jax
import jax.numpy as jnp
from jax import lax

S0 = 4096
S1 = 2048
S2 = 2048
BLK = 128


def symmetric_block(raw, factor, size):
    rise = 1.0 + 3.0 * jnp.arange(size, dtype=jnp.float32) / (size - 1)
    spread = (raw + raw.T) * (0.7071 / jnp.sqrt(jnp.float32(size)))
    eye = jnp.eye(size, dtype=jnp.float32)
    return spread * (1.0 - eye) + eye * (rise * factor)[None, :]


def draw_root_inverse(key, part):
    key = jax.random.fold_in(key, 1)
    first, second = jax.random.split(key)
    raw = jnp.clip(jax.random.normal(first, (S0, S0), jnp.float32), -5.0, 5.0)
    factor = jnp.exp(jax.random.uniform(second, (S0,), jnp.float32, jnp.log(1.5), jnp.log(3.0)))
    return symmetric_block(raw, factor, S0)


def draw_middle_inverse(key, part):
    key = jax.random.fold_in(key, 2)
    blocks = []
    for front in range(2):
        first, second = jax.random.split(jax.random.fold_in(key, 20 + front))
        raw = jnp.clip(jax.random.normal(first, (S1, S1), jnp.float32), -5.0, 5.0)
        factor = jnp.exp(jax.random.uniform(second, (S1,), jnp.float32, jnp.log(1.5), jnp.log(3.0)))
        blocks.append(symmetric_block(raw, factor, S1))
    return jnp.concatenate(blocks, axis=1)


def place_ends(result, own_key, smallest, high):
    dims = result.shape
    spot = [jax.random.randint(jax.random.fold_in(own_key, axis), (), 0, dims[axis]) for axis in range(len(dims))]
    result = result.at[tuple(spot)].set(smallest)
    longest = dims.index(max(dims))
    spot[longest] = (spot[longest] + 1) % dims[longest]
    return result.at[tuple(spot)].set(high)


def levels(stream_key, dims, cuts, low, top_value):
    def one(axis_at, shards_of):
        heights = jax.random.uniform(jax.random.fold_in(jax.random.fold_in(stream_key, 6), axis_at), (shards_of,), jnp.float32, low / len(cuts), top_value / len(cuts))
        return jnp.repeat(jnp.exp(heights), dims[axis_at] // shards_of).reshape((-1,) + (1,) * (len(dims) - axis_at - 1))

    factor_of = one(*cuts[0])
    for cut in cuts[1:]:
        factor_of = factor_of * one(*cut)
    return factor_of


def normal_values(own_key, dims, deviation, limit, pieces=(), kind=jnp.bfloat16):
    entries = deviation * jax.random.normal(own_key, dims, jnp.float32)
    if pieces:
        entries = entries * levels(own_key, dims, pieces, -0.22, 0.18)
    return jnp.clip(entries, -limit, limit).astype(kind)


def setup_inputs(seed: int = 0) -> dict:
    streams_of = jax.random.split(jax.random.key(seed), 8)
    return {
        "root_inverse": draw_root_inverse(jax.random.fold_in(streams_of[7], 71), 0),
        "middle_inverse": draw_middle_inverse(jax.random.fold_in(streams_of[7], 71), 0),
        "middle_panel": normal_values(streams_of[2], (S0, 2 * S1), (S0 // 4) ** -0.5, 0.1875, ((0, 8), (1, 4)), jnp.float32),
        "lower_root": normal_values(streams_of[3], (S0, 4 * S2), (S0 // 4) ** -0.5, 0.1875, ((0, 8), (1, 4)), jnp.float32),
        "lower_middle": normal_values(streams_of[4], (S1, 4 * S2), (S1 // 4) ** -0.5, 0.25, ((1, 4),), jnp.float32),
        "block_pattern": place_ends((jax.random.randint(streams_of[5], (4, S0 // BLK), 0, 3) < 2).astype(jnp.int32), jax.random.fold_in(streams_of[5], 1), 0, 1),
        "lower_diagonal": jnp.clip(jnp.exp(math.log(6.0) - 1.3862944 * jax.random.uniform(streams_of[6], (4 * S2,), jnp.float32) ** levels(streams_of[6], (4 * S2,), ((0, 4),), -0.2, 0.2)), 1.5, 6.0),
    }


def reference(root_inverse, middle_inverse, middle_panel, lower_root, lower_middle, block_pattern, lower_diagonal):
    exact = lax.Precision.HIGHEST
    keep = jnp.repeat(block_pattern.astype(jnp.float32), BLK, axis=1)
    first_side = jnp.dot(root_inverse, middle_panel, precision=exact, preferred_element_type=jnp.float32)
    diagonals = []
    for front in range(2):
        diagonals.append(jnp.diagonal(middle_inverse[:, front * S1:(front + 1) * S1]))
    middle_variance = jnp.concatenate(diagonals) + jnp.sum(middle_panel * first_side, axis=0)
    crosses = []
    parents = []
    lowers = []
    for front in range(4):
        parent = front // 2
        columns = slice(front * S2, (front + 1) * S2)
        parent_columns = slice(parent * S1, (parent + 1) * S1)
        lower_panel = lower_root[:, columns] * keep[front][:, None]
        reduced = lower_panel - jnp.dot(middle_panel[:, parent_columns], lower_middle[:, columns], precision=exact, preferred_element_type=jnp.float32)
        root_side = jnp.dot(root_inverse, reduced, precision=exact, preferred_element_type=jnp.float32)
        parent_side = jnp.dot(middle_inverse[:, parent_columns], lower_middle[:, columns], precision=exact, preferred_element_type=jnp.float32)
        parent_side = parent_side - jnp.dot(middle_panel[:, parent_columns].T, root_side, precision=exact, preferred_element_type=jnp.float32)
        lowers.append(lower_diagonal[columns] + jnp.sum(lower_panel * root_side, axis=0) + jnp.sum(lower_middle[:, columns] * parent_side, axis=0))
        crosses.append(root_side)
        parents.append(parent_side)
    lower_cross = -jnp.concatenate(crosses, axis=1)
    lower_parent = -jnp.concatenate(parents, axis=1)
    return (-first_side, middle_variance, lower_cross, lower_parent, jnp.concatenate(lowers))
```

```python
import functools

import jax
import jax.numpy as jnp
from jax import lax
from jax.experimental import pallas as pl
from jax.experimental.pallas import tpu as pltpu
from jax.sharding import PartitionSpec as P

BLK = 128


near = lax.Precision.HIGH


def dot(left, right):
    return lax.dot_general(
        left, right, (((1,), (0,)), ((), ())), precision=near, preferred_element_type=jnp.float32
    )


def split(value):
    high = value.astype(jnp.bfloat16)
    return high, (value - high.astype(jnp.float32)).astype(jnp.bfloat16)


def split_dot(left_high, left_low, right_high, right_low):
    def one(left, right):
        return jnp.dot(left, right, preferred_element_type=jnp.float32)

    return one(left_high, right_high) + (one(left_high, right_low) + one(left_low, right_high))


def split_blocks(block_refs, high_ref, low_ref):
    start = 0
    for block_ref in block_refs:
        place = slice(start, start + block_ref.shape[0])
        high_ref[place, :], low_ref[place, :] = split(block_ref[...])
        start += block_ref.shape[0]


def root_kernel(count, index_ref, root_ref, *refs):
    block_refs, out_ref = refs[:-5], refs[-5]
    root_high, root_low, high, low = refs[-4:]
    rows = root_ref.shape[1] // count

    @pl.when(pl.program_id(0) == 0)
    def _():
        for e in range(count):
            place = slice(e * rows, (e + 1) * rows)
            start = pl.multiple_of((index_ref[0] ^ e) * rows, rows)
            root_high[:, place], root_low[:, place] = split(root_ref[:, pl.ds(start, rows)])

    split_blocks(block_refs, high, low)
    out_ref[...] = split_dot(root_high[...], root_low[...], high[...], low[...])


def side_kernel(count, *refs):
    column_refs, block_refs, out_ref = refs[:count], refs[count:-5], refs[-5]
    side_high, side_low, high, low = refs[-4:]

    @pl.when(pl.program_id(0) == 0)
    def _():
        start = 0
        for column_ref in column_refs:
            place = slice(start, start + column_ref.shape[0])
            start += column_ref.shape[0]
            side_high[:, place], side_low[:, place] = split(column_ref[...].T)

    split_blocks(block_refs, high, low)
    out_ref[...] = split_dot(side_high[...], side_low[...], high[...], low[...])


def panel_scratch(height, depth, tile):
    return [
        pltpu.VMEM((height, depth), jnp.bfloat16),
        pltpu.VMEM((height, depth), jnp.bfloat16),
        pltpu.VMEM((depth, tile), jnp.bfloat16),
        pltpu.VMEM((depth, tile), jnp.bfloat16),
    ]


def panel_cost(height, depth, width):
    return pl.CostEstimate(
        flops=6 * height * depth * width,
        transcendentals=0,
        bytes_accessed=4 * (height * depth + depth * width + height * width),
    )


def whole_spec(array, index):
    return pl.BlockSpec(array.shape, index, pipeline_mode=pl.Buffered(1))


def root_times(index, root_rows, blocks, row=0, rows=1):
    height, depth = root_rows.shape[0] // rows, root_rows.shape[1]
    count = lax.axis_size("grid")
    width = blocks[0].shape[1]
    tile = min(width, 256)
    return pl.pallas_call(
        functools.partial(root_kernel, count),
        grid_spec=pltpu.PrefetchScalarGridSpec(
            num_scalar_prefetch=1,
            grid=(width // tile,),
            in_specs=[
                pl.BlockSpec(
                    (height, depth), lambda i, s: (row, 0), pipeline_mode=pl.Buffered(1)
                )
            ]
            + [pl.BlockSpec((block.shape[0], tile), lambda i, s: (0, i)) for block in blocks],
            out_specs=pl.BlockSpec((height, tile), lambda i, s: (0, i)),
            scratch_shapes=panel_scratch(height, depth, tile),
        ),
        out_shape=jax.ShapeDtypeStruct((height, width), jnp.float32),
        compiler_params=pltpu.CompilerParams(vmem_limit_bytes=44 * 2**20),
        cost_estimate=panel_cost(height, depth, width),
    )(index, root_rows, *blocks)


def side_times(columns, blocks):
    height = columns[0].shape[1]
    depth = sum(block.shape[0] for block in blocks)
    width = blocks[0].shape[1]
    tile = min(width, 256)
    return pl.pallas_call(
        functools.partial(side_kernel, len(columns)),
        grid=(width // tile,),
        in_specs=[whole_spec(column, lambda i: (0, 0)) for column in columns]
        + [pl.BlockSpec((block.shape[0], tile), lambda i: (0, i)) for block in blocks],
        out_specs=pl.BlockSpec((height, tile), lambda i: (0, i)),
        scratch_shapes=panel_scratch(height, depth, tile),
        out_shape=jax.ShapeDtypeStruct((height, width), jnp.float32),
        compiler_params=pltpu.CompilerParams(vmem_limit_bytes=44 * 2**20),
        cost_estimate=panel_cost(height, depth, width),
    )(*columns, *blocks)


def after(value, other):
    return lax.optimization_barrier((value, other))[0]


def swap(value, axis, flip):
    count = lax.axis_size(axis)
    return lax.ppermute(value, axis, [(i, i ^ flip) for i in range(count)])


def gather_chips(own, before=()):
    half = own.shape[0] // 2
    across, along, core = swap(own, "grid", 2), swap(own, "grid", 4), swap(own, "grid", 1)
    held = after([across, along], (core, before))
    onward = [held[0][:half], held[1][half:]]
    diagonal = [swap(onward[0], "grid", 4), swap(onward[1], "grid", 2)]
    blocks = {0: [own], 1: [core], 2: [across], 4: [along], 6: diagonal}
    blocks[3], blocks[5] = [swap(across, "grid", 1)], [swap(along, "grid", 1)]
    return blocks, onward


def doubled_hops(own):
    blocks, flip = {0: [own]}, 2
    while flip < lax.axis_size("grid"):
        for e in list(blocks):
            blocks[e | flip] = [swap(part, "grid", flip) for part in blocks[e]]
        flip *= 2
    return blocks


def gather_cores(blocks):
    for e in list(blocks):
        if e | 1 not in blocks:
            blocks[e | 1] = [swap(part, "grid", 1) for part in blocks[e]]
    return [part for e in range(len(blocks)) for part in blocks[e]]


def local(
    root_inverse,
    middle_inverse,
    middle_panel,
    lower_root,
    lower_middle,
    block_pattern,
    lower_diagonal,
):
    leaf_count = lax.axis_size("leaf")
    grid_count = lax.axis_size("grid")
    leaf_index = lax.axis_index("leaf")
    grid_index = lax.axis_index("grid")
    siblings = leaf_count // 2
    sibling_index = leaf_index % siblings
    child_front = leaf_index // (leaf_count // 4)
    local_rows = lower_root.shape[0]
    own_columns = middle_inverse.shape[1]
    middle_count = middle_inverse.shape[0]

    square = grid_count == 8
    index = grid_index.astype(jnp.int32).reshape((1,))
    width = lower_root.shape[1]
    chunk = min(width, 1024)
    chunks = range(width // chunk)

    def middle_rows(s):
        return lax.dynamic_slice_in_dim(
            lower_middle, (sibling_index ^ s) * own_columns, own_columns, 0
        )

    blocks_here = local_rows // BLK
    pattern = lax.dynamic_slice(
        block_pattern, (child_front, grid_index * blocks_here), (1, blocks_here)
    )
    keep = jnp.repeat(pattern[0].astype(jnp.float32), BLK)
    lower_panel = lower_root * keep[:, None]
    root_rows = lax.all_gather(root_inverse, "leaf", axis=1, tiled=True)
    panels = [lower_panel[:, c * chunk : (c + 1) * chunk] for c in chunks]
    if square:
        middle_blocks, _ = gather_chips(middle_panel)
        first_blocks, _ = gather_chips(panels[0])
        near_by = [first_blocks[e] for e in (3, 5)]
    else:
        middle_blocks = doubled_hops(middle_panel)
        first_blocks, near_by = doubled_hops(panels[0]), []
    middle_blocks = gather_cores(middle_blocks)
    lower_blocks = [gather_cores(first_blocks)]
    panels[1:] = after(panels[1:], (middle_blocks, near_by))
    ready = after(root_rows, panels[1:])
    first_halves = [root_times(index, ready, middle_blocks, 0, 2)]
    ready = after(ready, first_halves)
    first_halves.append(root_times(index, ready, middle_blocks, 1, 2))
    for panel in panels[1:]:
        if square:
            blocks, onward = gather_chips(panel, (lower_blocks, first_halves))
            ready = after(ready, onward)
        else:
            blocks = doubled_hops(panel)
        lower_blocks.append(gather_cores(blocks))
    root_sides = [root_times(index, ready, lower_blocks[0])]

    def transposed(piece, parts):
        count = piece.shape[0]
        stacked = jnp.stack(parts, axis=0)

        def columns_for(flip):
            start = (grid_index ^ flip) * middle_count
            place = (start // own_columns) ^ sibling_index
            return lax.dynamic_slice(
                stacked, (place, 0, start % own_columns), (1, count, middle_count)
            )[0]

        chips = range(0, grid_count, 2)
        other_core = swap(jnp.concatenate([columns_for(e | 1) for e in chips], axis=0), "grid", 1)
        outgoing = [
            jnp.concatenate([columns_for(e), other_core[k * count : (k + 1) * count]], axis=0)
            for k, e in enumerate(chips)
        ]
        received = outgoing[:1] + [swap(outgoing[k], "grid", 2 * k) for k in range(1, len(chips))]
        return outgoing, [part for pair in received for part in (pair[:count], pair[count:])]

    sent = [
        [half] + [swap(half, "leaf", s) for s in range(1, siblings)] for half in first_halves
    ]
    sent[0] = after(sent[0], root_sides)
    outgoing, upper_columns = transposed(first_halves[0], sent[0])
    first_side = jnp.concatenate(first_halves, axis=0)
    root_own = dot(after(first_side, outgoing), middle_rows(0))
    sent[1] = after(sent[1], root_own)
    outgoing, lower_columns = transposed(first_halves[1], sent[1])
    ready = after(root_rows, outgoing)
    root_sides += [root_times(index, ready, blocks) for blocks in lower_blocks[1:]]
    root_side = jnp.concatenate(root_sides, axis=1) - root_own
    for s in range(1, siblings):
        other = jnp.concatenate([sent[0][s], sent[1][s]], axis=0)
        root_side = root_side - dot(other, middle_rows(s))

    side_columns = [part for pair in zip(upper_columns, lower_columns) for part in pair]
    shared = middle_inverse + side_times(side_columns, middle_blocks)
    shared_parts = [shared] + [swap(shared, "leaf", s) for s in range(1, siblings)]
    side_columns = after(side_columns, shared)
    side_products = [side_times(side_columns, blocks) for blocks in lower_blocks]
    parent_side = -jnp.concatenate(side_products, axis=1)
    for s in range(siblings):
        parent_side = parent_side + dot(shared_parts[s], middle_rows(s))

    global_rows = grid_index * middle_count + jnp.arange(middle_count, dtype=jnp.int32)
    global_columns = sibling_index * own_columns + jnp.arange(own_columns, dtype=jnp.int32)
    on_diagonal = global_rows[:, None] == global_columns[None, :]
    middle_part = jnp.sum(jnp.where(on_diagonal, middle_inverse, 0.0), axis=0) + jnp.sum(
        middle_panel * first_side, axis=0
    )
    lower_rows = lax.dynamic_slice_in_dim(lower_middle, grid_index * middle_count, middle_count, 0)
    lower_part = jnp.sum(lower_panel * root_side, axis=0) + jnp.sum(
        lower_rows * parent_side, axis=0
    )

    total = jnp.concatenate([middle_part, lower_part])
    flip = 1
    while flip < grid_count:
        total = total + swap(total, "grid", flip)
        flip *= 2
    middle_total = total[:own_columns]
    lower_total = total[own_columns:]
    return (-first_side, middle_total, -root_side, -parent_side, lower_diagonal + lower_total)


def solution(mesh):
    in_specs = (
        P("grid", "leaf"),
        P("grid", "leaf"),
        P("grid", "leaf"),
        P("grid", "leaf"),
        P(None, "leaf"),
        P(),
        P("leaf"),
    )
    out_specs = (P("grid", "leaf"), P("leaf"), P("grid", "leaf"), P("grid", "leaf"), P("leaf"))
    return jax.shard_map(local, mesh=mesh, in_specs=in_specs, out_specs=out_specs, check_vma=False)
```

```python
import functools

import jax
import jax.numpy as jnp
from jax import lax
from jax.experimental import pallas as pl
from jax.experimental.pallas import tpu as pltpu
from jax.sharding import PartitionSpec as P

BLK = 128


unhidden = pl.CostEstimate(flops=0, transcendentals=0, bytes_accessed=0)


def split(value):
    high = value.astype(jnp.bfloat16)
    return high, (value - high.astype(jnp.float32)).astype(jnp.bfloat16)


def split_dot(left_high, left_low, right_high, right_low):
    def one(left, right):
        return jnp.dot(left, right, preferred_element_type=jnp.float32)

    return one(left_high, right_high) + (one(left_high, right_low) + one(left_low, right_high))


def split_blocks(block_refs, high_ref, low_ref):
    start = 0
    for block_ref in block_refs:
        place = slice(start, start + block_ref.shape[0])
        high_ref[place, :], low_ref[place, :] = split(block_ref[...])
        start += block_ref.shape[0]


def root_kernel(count, index_ref, root_ref, *refs):
    block_refs, out_ref = refs[:-5], refs[-5]
    root_high, root_low, high, low = refs[-4:]
    rows = root_ref.shape[1] // count

    @pl.when(pl.program_id(0) == 0)
    def _():
        for e in range(count):
            place = slice(e * rows, (e + 1) * rows)
            start = pl.multiple_of((index_ref[0] ^ e) * rows, rows)
            root_high[:, place], root_low[:, place] = split(root_ref[:, pl.ds(start, rows)])

    split_blocks(block_refs, high, low)
    out_ref[...] = split_dot(root_high[...], root_low[...], high[...], low[...])


def side_kernel(count, *refs):
    column_refs, block_refs, out_ref = refs[:count], refs[count:-5], refs[-5]
    side_high, side_low, high, low = refs[-4:]

    @pl.when(pl.program_id(0) == 0)
    def _():
        rows = column_refs[0].shape[0] // 2
        for j, column_ref in enumerate(column_refs):
            for core in range(2):
                start = (2 * (j // 2) + core) * 2 * rows + (j % 2) * rows
                place = slice(start, start + rows)
                side_high[:, place], side_low[:, place] = split(
                    column_ref[core * rows : (core + 1) * rows, :].T
                )

    split_blocks(block_refs, high, low)
    out_ref[...] = split_dot(side_high[...], side_low[...], high[...], low[...])


def pick_kernel(parts, spot_ref, *refs):
    part_refs, out_refs = refs[:parts], refs[parts:]
    rows = part_refs[0].shape[0]
    width = out_refs[0].shape[1]
    spots = out_refs[0].shape[0] // rows
    for j in range(2 * spots):
        band = slice((j // 2) * rows, (j // 2 + 1) * rows)
        column = pl.multiple_of(spot_ref[2 * j + 1], width)
        for s in range(parts):

            @pl.when(spot_ref[2 * j] == s)
            def _():
                out_refs[j % 2][band, :] = part_refs[s][:, pl.ds(column, width)]


def pick(spots, parts, width):
    rows = parts[0].shape[0]
    shape = jax.ShapeDtypeStruct((spots.shape[0] // 4 * rows, width), jnp.float32)
    whole = pl.BlockSpec(memory_space=pltpu.VMEM)
    return pl.pallas_call(
        functools.partial(pick_kernel, len(parts)),
        in_specs=[pl.BlockSpec(memory_space=pltpu.SMEM)] + [whole] * len(parts),
        out_specs=[whole, whole],
        out_shape=[shape, shape],
        compiler_params=pltpu.CompilerParams(vmem_limit_bytes=32 * 2**20),
        cost_estimate=unhidden,
    )(spots, *parts)


def pair_kernel(kept_ref, taken_ref, *out_refs):
    rows = out_refs[0].shape[0] // 2
    for k, out_ref in enumerate(out_refs):
        band = slice(k * rows, (k + 1) * rows)
        out_ref[:rows, :] = kept_ref[band, :]
        out_ref[rows:, :] = taken_ref[band, :]


def pair(kept, taken, count):
    shape = jax.ShapeDtypeStruct((2 * kept.shape[0] // count, kept.shape[1]), jnp.float32)
    whole = pl.BlockSpec(memory_space=pltpu.VMEM)
    return pl.pallas_call(
        pair_kernel,
        in_specs=[whole, whole],
        out_specs=[whole] * count,
        out_shape=[shape] * count,
        compiler_params=pltpu.CompilerParams(vmem_limit_bytes=32 * 2**20),
        cost_estimate=unhidden,
    )(kept, taken)


def panel_scratch(height, depth, tile):
    return [
        pltpu.VMEM((height, depth), jnp.bfloat16),
        pltpu.VMEM((height, depth), jnp.bfloat16),
        pltpu.VMEM((depth, tile), jnp.bfloat16),
        pltpu.VMEM((depth, tile), jnp.bfloat16),
    ]


def whole_spec(array, index):
    return pl.BlockSpec(array.shape, index, pipeline_mode=pl.Buffered(1))


def root_times(index, root_rows, blocks, row=0, rows=1):
    height, depth = root_rows.shape[0] // rows, root_rows.shape[1]
    count = lax.axis_size("grid")
    width = blocks[0].shape[1]
    tile = min(width, 256)
    return pl.pallas_call(
        functools.partial(root_kernel, count),
        grid_spec=pltpu.PrefetchScalarGridSpec(
            num_scalar_prefetch=1,
            grid=(width // tile,),
            in_specs=[
                pl.BlockSpec(
                    (height, depth), lambda i, s: (row, 0), pipeline_mode=pl.Buffered(1)
                )
            ]
            + [pl.BlockSpec((block.shape[0], tile), lambda i, s: (0, i)) for block in blocks],
            out_specs=pl.BlockSpec((height, tile), lambda i, s: (0, i)),
            scratch_shapes=panel_scratch(height, depth, tile),
        ),
        out_shape=jax.ShapeDtypeStruct((height, width), jnp.float32),
        compiler_params=pltpu.CompilerParams(vmem_limit_bytes=44 * 2**20),
        cost_estimate=unhidden,
    )(index, root_rows, *blocks)


def side_times(columns, blocks):
    height = columns[0].shape[1]
    depth = sum(block.shape[0] for block in blocks)
    width = blocks[0].shape[1]
    tile = min(width, 256)
    return pl.pallas_call(
        functools.partial(side_kernel, len(columns)),
        grid=(width // tile,),
        in_specs=[whole_spec(column, lambda i: (0, 0)) for column in columns]
        + [pl.BlockSpec((block.shape[0], tile), lambda i: (0, i)) for block in blocks],
        out_specs=pl.BlockSpec((height, tile), lambda i: (0, i)),
        scratch_shapes=panel_scratch(height, depth, tile),
        out_shape=jax.ShapeDtypeStruct((height, width), jnp.float32),
        compiler_params=pltpu.CompilerParams(vmem_limit_bytes=44 * 2**20),
        cost_estimate=unhidden,
    )(*columns, *blocks)


def mixed_kernel(parts, pieces, places_ref, *refs):
    left_refs, right_refs, out_ref = refs[: parts * pieces], refs[parts * pieces : -5], refs[-5]
    left_high, left_low, high, low = refs[-4:]

    @pl.when(pl.program_id(0) == 0)
    def _():
        for s in range(parts):
            top = 0
            for left_ref in left_refs[s * pieces : (s + 1) * pieces]:
                count, depth = left_ref.shape
                band, place = slice(top, top + count), slice(s * depth, (s + 1) * depth)
                left_high[band, place], left_low[band, place] = split(left_ref[...])
                top += count

    split_blocks(right_refs, high, low)
    out_ref[...] = split_dot(left_high[...], left_low[...], high[...], low[...])


def mixed_times(places, left, right):
    height = sum(piece.shape[0] for piece in left[0])
    own = left[0][0].shape[1]
    depth, width = right.shape
    tile = min(width, 256)

    def band(s):
        return pl.BlockSpec((own, tile), lambda i, places: (places[s], i))

    return pl.pallas_call(
        functools.partial(mixed_kernel, len(left), len(left[0])),
        grid_spec=pltpu.PrefetchScalarGridSpec(
            num_scalar_prefetch=1,
            grid=(width // tile,),
            in_specs=[whole_spec(piece, lambda i, p: (0, 0)) for part in left for piece in part]
            + [band(s) for s in range(len(left))],
            out_specs=pl.BlockSpec((height, tile), lambda i, p: (0, i)),
            scratch_shapes=panel_scratch(height, depth, tile),
        ),
        out_shape=jax.ShapeDtypeStruct((height, width), jnp.float32),
        compiler_params=pltpu.CompilerParams(vmem_limit_bytes=44 * 2**20),
        cost_estimate=unhidden,
    )(places, *[piece for part in left for piece in part], *[right] * len(left))


def after(value, other):
    return lax.optimization_barrier((value, other))[0]


def swap(value, axis, flip):
    count = lax.axis_size(axis)
    return lax.ppermute(value, axis, [(i, i ^ flip) for i in range(count)])


def gather_chips(own, before=()):
    half = own.shape[0] // 2
    across, along, core = swap(own, "grid", 2), swap(own, "grid", 4), swap(own, "grid", 1)
    held = after([across, along], (core, before))
    onward = [held[0][:half], held[1][half:]]
    diagonal = [swap(onward[0], "grid", 4), swap(onward[1], "grid", 2)]
    blocks = {0: [own], 1: [core], 2: [across], 4: [along], 6: diagonal}
    blocks[3], blocks[5] = [swap(across, "grid", 1)], [swap(along, "grid", 1)]
    return blocks, onward


def doubled_hops(own):
    blocks, flip = {0: [own]}, 2
    while flip < lax.axis_size("grid"):
        for e in list(blocks):
            blocks[e | flip] = [swap(part, "grid", flip) for part in blocks[e]]
        flip *= 2
    return blocks


def gather_cores(blocks):
    for e in list(blocks):
        if e | 1 not in blocks:
            blocks[e | 1] = [swap(part, "grid", 1) for part in blocks[e]]
    return [part for e in range(len(blocks)) for part in blocks[e]]


def local(
    root_inverse,
    middle_inverse,
    middle_panel,
    lower_root,
    lower_middle,
    block_pattern,
    lower_diagonal,
):
    leaf_count = lax.axis_size("leaf")
    grid_count = lax.axis_size("grid")
    leaf_index = lax.axis_index("leaf")
    grid_index = lax.axis_index("grid")
    siblings = leaf_count // 2
    sibling_index = leaf_index % siblings
    child_front = leaf_index // (leaf_count // 4)
    local_rows = lower_root.shape[0]
    own_columns = middle_inverse.shape[1]
    middle_count = middle_inverse.shape[0]

    square = grid_count == 8
    index = grid_index.astype(jnp.int32).reshape((1,))
    width = lower_root.shape[1]
    chunk = min(width, 1024)
    chunks = range(width // chunk)

    places = jnp.stack([sibling_index ^ s for s in range(siblings)]).astype(jnp.int32)

    blocks_here = local_rows // BLK
    pattern = lax.dynamic_slice(
        block_pattern, (child_front, grid_index * blocks_here), (1, blocks_here)
    )
    keep = jnp.repeat(pattern[0].astype(jnp.float32), BLK)
    lower_panel = lower_root * keep[:, None]
    root_rows = lax.all_gather(root_inverse, "leaf", axis=1, tiled=True)
    panels = [lower_panel[:, c * chunk : (c + 1) * chunk] for c in chunks]
    if square:
        middle_blocks, _ = gather_chips(middle_panel)
        first_blocks, _ = gather_chips(panels[0])
        near_by = [first_blocks[e] for e in (3, 5)]
    else:
        middle_blocks = doubled_hops(middle_panel)
        first_blocks, near_by = doubled_hops(panels[0]), []
    middle_blocks = gather_cores(middle_blocks)
    lower_blocks = [gather_cores(first_blocks)]
    panels[1:] = after(panels[1:], (middle_blocks, near_by))
    ready = after(root_rows, (panels[1:], lower_blocks))
    first_halves = [root_times(index, ready, middle_blocks, 0, 2)]
    ready = after(ready, first_halves)
    first_halves.append(root_times(index, ready, middle_blocks, 1, 2))
    arrived = [first_halves[1]]
    for panel in panels[1:]:
        if square:
            blocks, _ = gather_chips(panel, (lower_blocks, first_halves))
            arrived += [blocks[e] for e in (1, 2, 4)]
        else:
            blocks = doubled_hops(panel)
        lower_blocks.append(gather_cores(blocks))

    spots = []
    for e in range(grid_count):
        start = (grid_index ^ e) * middle_count
        spots += [(start // own_columns) ^ sibling_index, start % own_columns]
    spots = jnp.stack(spots).astype(jnp.int32)

    def transposed(parts):
        kept, other = pick(spots, parts, middle_count)
        outgoing = pair(kept, swap(other, "grid", 1), grid_count // 2)
        return outgoing, [outgoing[0]] + [
            swap(outgoing[k], "grid", 2 * k) for k in range(1, len(outgoing))
        ]

    sent = [
        [half] + [swap(half, "leaf", s) for s in range(1, siblings)] for half in first_halves
    ]
    sent[0] = after(sent[0], arrived)
    outgoing, upper_columns = transposed(sent[0])
    ready = after(root_rows, outgoing)
    root_sides = [root_times(index, ready, lower_blocks[0])]
    sent[1] = after(sent[1], root_sides)
    outgoing, lower_columns = transposed(sent[1])
    first_side = jnp.concatenate(first_halves, axis=0)
    left = [[sent[0][s], sent[1][s]] for s in range(siblings)]
    mixed = mixed_times(places, after(left, outgoing), lower_middle)
    ready = after(root_rows, mixed)
    root_sides += [root_times(index, ready, blocks) for blocks in lower_blocks[1:]]
    root_side = jnp.concatenate(root_sides, axis=1) - mixed

    side_columns = [part for pair in zip(upper_columns, lower_columns) for part in pair]
    side_columns = after(side_columns, root_sides)
    shared = middle_inverse + side_times(side_columns, middle_blocks)
    shared_parts = [[shared]] + [[swap(shared, "leaf", s)] for s in range(1, siblings)]
    side_columns = after(side_columns, shared)
    side_products = [side_times(side_columns, blocks) for blocks in lower_blocks]
    shared_parts = after(shared_parts, side_products)
    parent_side = mixed_times(places, shared_parts, lower_middle) - jnp.concatenate(
        side_products, axis=1
    )

    global_rows = grid_index * middle_count + jnp.arange(middle_count, dtype=jnp.int32)
    global_columns = sibling_index * own_columns + jnp.arange(own_columns, dtype=jnp.int32)
    on_diagonal = global_rows[:, None] == global_columns[None, :]
    middle_part = jnp.sum(jnp.where(on_diagonal, middle_inverse, 0.0), axis=0) + jnp.sum(
        middle_panel * first_side, axis=0
    )
    lower_rows = lax.dynamic_slice_in_dim(lower_middle, grid_index * middle_count, middle_count, 0)
    lower_part = jnp.sum(lower_panel * root_side, axis=0) + jnp.sum(
        lower_rows * parent_side, axis=0
    )

    total = jnp.concatenate([middle_part, lower_part])
    flip = 1
    while flip < grid_count:
        total = total + swap(total, "grid", flip)
        flip *= 2
    middle_total = total[:own_columns]
    lower_total = total[own_columns:]
    return (-first_side, middle_total, -root_side, -parent_side, lower_diagonal + lower_total)


def solution(mesh):
    in_specs = (
        P("grid", "leaf"),
        P("grid", "leaf"),
        P("grid", "leaf"),
        P("grid", "leaf"),
        P(None, "leaf"),
        P(),
        P("leaf"),
    )
    out_specs = (P("grid", "leaf"), P("leaf"), P("grid", "leaf"), P("grid", "leaf"), P("leaf"))
    return jax.shard_map(local, mesh=mesh, in_specs=in_specs, out_specs=out_specs, check_vma=False)
```

```python
import functools

import jax
import jax.numpy as jnp
from jax import lax
from jax.experimental import pallas as pl
from jax.experimental.pallas import tpu as pltpu
from jax.sharding import PartitionSpec as P

BLK = 128


unhidden = pl.CostEstimate(flops=0, transcendentals=0, bytes_accessed=0)


def split(value):
    high = value.astype(jnp.bfloat16)
    return high, (value - high.astype(jnp.float32)).astype(jnp.bfloat16)


def split_dot(left_high, left_low, right_high, right_low):
    def one(left, right):
        return jnp.dot(left, right, preferred_element_type=jnp.float32)

    return one(left_high, right_high) + (one(left_high, right_low) + one(left_low, right_high))


def split_blocks(block_refs, high_ref, low_ref):
    start = 0
    for block_ref in block_refs:
        place = slice(start, start + block_ref.shape[0])
        high_ref[place, :], low_ref[place, :] = split(block_ref[...])
        start += block_ref.shape[0]


def root_kernel(count, index_ref, root_ref, *refs):
    block_refs, out_ref = refs[:-5], refs[-5]
    root_high, root_low, high, low = refs[-4:]
    rows = root_ref.shape[1] // count

    @pl.when(pl.program_id(0) == 0)
    def _():
        for e in range(count):
            place = slice(e * rows, (e + 1) * rows)
            start = pl.multiple_of((index_ref[0] ^ e) * rows, rows)
            root_high[:, place], root_low[:, place] = split(root_ref[:, pl.ds(start, rows)])

    split_blocks(block_refs, high, low)
    out_ref[...] = split_dot(root_high[...], root_low[...], high[...], low[...])


def side_kernel(count, *refs):
    column_refs, block_refs, out_ref = refs[:count], refs[count:-5], refs[-5]
    side_high, side_low, high, low = refs[-4:]

    @pl.when(pl.program_id(0) == 0)
    def _():
        rows = column_refs[0].shape[0] // 2
        for j, column_ref in enumerate(column_refs):
            for core in range(2):
                start = (2 * (j // 2) + core) * 2 * rows + (j % 2) * rows
                place = slice(start, start + rows)
                side_high[:, place], side_low[:, place] = split(
                    column_ref[core * rows : (core + 1) * rows, :].T
                )

    split_blocks(block_refs, high, low)
    out_ref[...] = split_dot(side_high[...], side_low[...], high[...], low[...])


def pick_kernel(parts, spot_ref, *refs):
    part_refs, out_refs = refs[:parts], refs[parts:]
    rows = part_refs[0].shape[0]
    width = out_refs[0].shape[1]
    spots = out_refs[0].shape[0] // rows
    for j in range(2 * spots):
        band = slice((j // 2) * rows, (j // 2 + 1) * rows)
        column = pl.multiple_of(spot_ref[2 * j + 1], width)
        for s in range(parts):

            @pl.when(spot_ref[2 * j] == s)
            def _():
                out_refs[j % 2][band, :] = part_refs[s][:, pl.ds(column, width)]


def pick(spots, parts, width):
    rows = parts[0].shape[0]
    shape = jax.ShapeDtypeStruct((spots.shape[0] // 4 * rows, width), jnp.float32)
    whole = pl.BlockSpec(memory_space=pltpu.VMEM)
    return pl.pallas_call(
        functools.partial(pick_kernel, len(parts)),
        in_specs=[pl.BlockSpec(memory_space=pltpu.SMEM)] + [whole] * len(parts),
        out_specs=[whole, whole],
        out_shape=[shape, shape],
        compiler_params=pltpu.CompilerParams(vmem_limit_bytes=32 * 2**20),
        cost_estimate=unhidden,
    )(spots, *parts)


def pair_kernel(kept_ref, taken_ref, *out_refs):
    rows = out_refs[0].shape[0] // 2
    for k, out_ref in enumerate(out_refs):
        band = slice(k * rows, (k + 1) * rows)
        out_ref[:rows, :] = kept_ref[band, :]
        out_ref[rows:, :] = taken_ref[band, :]


def pair(kept, taken, count):
    shape = jax.ShapeDtypeStruct((2 * kept.shape[0] // count, kept.shape[1]), jnp.float32)
    whole = pl.BlockSpec(memory_space=pltpu.VMEM)
    return pl.pallas_call(
        pair_kernel,
        in_specs=[whole, whole],
        out_specs=[whole] * count,
        out_shape=[shape] * count,
        compiler_params=pltpu.CompilerParams(vmem_limit_bytes=32 * 2**20),
        cost_estimate=unhidden,
    )(kept, taken)


def panel_scratch(height, depth, tile):
    return [
        pltpu.VMEM((height, depth), jnp.bfloat16),
        pltpu.VMEM((height, depth), jnp.bfloat16),
        pltpu.VMEM((depth, tile), jnp.bfloat16),
        pltpu.VMEM((depth, tile), jnp.bfloat16),
    ]


def whole_spec(array, index):
    return pl.BlockSpec(array.shape, index, pipeline_mode=pl.Buffered(1))


def root_times(index, root_rows, blocks, row=0, rows=1):
    height, depth = root_rows.shape[0] // rows, root_rows.shape[1]
    count = lax.axis_size("grid")
    width = blocks[0].shape[1]
    tile = min(width, 256)
    return pl.pallas_call(
        functools.partial(root_kernel, count),
        grid_spec=pltpu.PrefetchScalarGridSpec(
            num_scalar_prefetch=1,
            grid=(width // tile,),
            in_specs=[
                pl.BlockSpec(
                    (height, depth), lambda i, s: (row, 0), pipeline_mode=pl.Buffered(1)
                )
            ]
            + [pl.BlockSpec((block.shape[0], tile), lambda i, s: (0, i)) for block in blocks],
            out_specs=pl.BlockSpec((height, tile), lambda i, s: (0, i)),
            scratch_shapes=panel_scratch(height, depth, tile),
        ),
        out_shape=jax.ShapeDtypeStruct((height, width), jnp.float32),
        compiler_params=pltpu.CompilerParams(vmem_limit_bytes=44 * 2**20),
        cost_estimate=unhidden,
    )(index, root_rows, *blocks)


def side_times(columns, blocks):
    height = columns[0].shape[1]
    depth = sum(block.shape[0] for block in blocks)
    width = blocks[0].shape[1]
    tile = min(width, 256)
    return pl.pallas_call(
        functools.partial(side_kernel, len(columns)),
        grid=(width // tile,),
        in_specs=[whole_spec(column, lambda i: (0, 0)) for column in columns]
        + [pl.BlockSpec((block.shape[0], tile), lambda i: (0, i)) for block in blocks],
        out_specs=pl.BlockSpec((height, tile), lambda i: (0, i)),
        scratch_shapes=panel_scratch(height, depth, tile),
        out_shape=jax.ShapeDtypeStruct((height, width), jnp.float32),
        compiler_params=pltpu.CompilerParams(vmem_limit_bytes=44 * 2**20),
        cost_estimate=unhidden,
    )(*columns, *blocks)


def mixed_kernel(parts, pieces, places_ref, *refs):
    left_refs, refs = refs[: parts * pieces], refs[parts * pieces :]
    right_refs, refs = refs[:parts], refs[parts:]
    left_high, left_low, high, low = refs[-4:]

    @pl.when(pl.program_id(0) == 0)
    def _():
        for s in range(parts):
            top = 0
            for left_ref in left_refs[s * pieces : (s + 1) * pieces]:
                count, depth = left_ref.shape
                band, place = slice(top, top + count), slice(s * depth, (s + 1) * depth)
                left_high[band, place], left_low[band, place] = split(left_ref[...])
                top += count

    split_blocks(right_refs, high, low)
    product = split_dot(left_high[...], left_low[...], high[...], low[...])
    if len(refs) == 5:
        refs[0][...] = product
        return
    side_refs, (rows_ref, out_ref, sums_ref) = refs[:-7], refs[-7:-4]
    for c, side_ref in enumerate(side_refs):

        @pl.when(pl.program_id(0) // (pl.num_programs(0) // len(side_refs)) == c)
        def _():
            negative = side_ref[...] - product
            out_ref[...] = negative
            sums_ref[...] = -jnp.sum(rows_ref[...] * negative, axis=0, keepdims=True)


def mixed_times(places, left, right, sides=()):
    height = sum(piece.shape[0] for piece in left[0])
    own = left[0][0].shape[1]
    depth, width = right.shape
    tile = min(width, 256)
    out_specs = [pl.BlockSpec((height, tile), lambda i, p: (0, i))]
    out_shape = [jax.ShapeDtypeStruct((height, width), jnp.float32)]
    extra, extra_specs = [], []
    if sides:
        tiles = width // tile // len(sides)

        def part(c):
            def place(i, places):
                return 0, jnp.clip(i - c * tiles, 0, tiles - 1)

            return pl.BlockSpec((height, tile), place)

        extra = [*sides, right]
        extra_specs = [part(c) for c in range(len(sides))] + [
            pl.BlockSpec((height, tile), lambda i, places: (places[len(left)], i))
        ]
        out_specs = out_specs + [pl.BlockSpec((1, tile), lambda i, p: (0, i))]
        out_shape = out_shape + [jax.ShapeDtypeStruct((1, width), jnp.float32)]

    def band(s):
        return pl.BlockSpec((own, tile), lambda i, places: (places[s], i))

    return pl.pallas_call(
        functools.partial(mixed_kernel, len(left), len(left[0])),
        grid_spec=pltpu.PrefetchScalarGridSpec(
            num_scalar_prefetch=1,
            grid=(width // tile,),
            in_specs=[whole_spec(piece, lambda i, p: (0, 0)) for part in left for piece in part]
            + [band(s) for s in range(len(left))]
            + extra_specs,
            out_specs=out_specs,
            scratch_shapes=panel_scratch(height, depth, tile),
        ),
        out_shape=out_shape,
        compiler_params=pltpu.CompilerParams(vmem_limit_bytes=44 * 2**20),
        cost_estimate=unhidden,
    )(places, *[piece for part in left for piece in part], *[right] * len(left), *extra)


def after(value, other):
    return lax.optimization_barrier((value, other))[0]


def swap(value, axis, flip):
    count = lax.axis_size(axis)
    return lax.ppermute(value, axis, [(i, i ^ flip) for i in range(count)])


def gather_chips(own, before=()):
    half = own.shape[0] // 2
    across, along, core = swap(own, "grid", 2), swap(own, "grid", 4), swap(own, "grid", 1)
    held = after([across, along], (core, before))
    onward = [held[0][:half], held[1][half:]]
    diagonal = [swap(onward[0], "grid", 4), swap(onward[1], "grid", 2)]
    blocks = {0: [own], 1: [core], 2: [across], 4: [along], 6: diagonal}
    blocks[3], blocks[5] = [swap(across, "grid", 1)], [swap(along, "grid", 1)]
    return blocks, onward


def doubled_hops(own):
    blocks, flip = {0: [own]}, 2
    while flip < lax.axis_size("grid"):
        for e in list(blocks):
            blocks[e | flip] = [swap(part, "grid", flip) for part in blocks[e]]
        flip *= 2
    return blocks


def gather_cores(blocks):
    for e in list(blocks):
        if e | 1 not in blocks:
            blocks[e | 1] = [swap(part, "grid", 1) for part in blocks[e]]
    return [part for e in range(len(blocks)) for part in blocks[e]]


def local(
    root_inverse,
    middle_inverse,
    middle_panel,
    lower_root,
    lower_middle,
    block_pattern,
    lower_diagonal,
):
    leaf_count = lax.axis_size("leaf")
    grid_count = lax.axis_size("grid")
    leaf_index = lax.axis_index("leaf")
    grid_index = lax.axis_index("grid")
    siblings = leaf_count // 2
    sibling_index = leaf_index % siblings
    child_front = leaf_index // (leaf_count // 4)
    local_rows = lower_root.shape[0]
    own_columns = middle_inverse.shape[1]
    middle_count = middle_inverse.shape[0]

    square = grid_count == 8
    index = grid_index.astype(jnp.int32).reshape((1,))
    width = lower_root.shape[1]
    chunk = min(width, 1024)
    chunks = range(width // chunk)

    places = [sibling_index ^ s for s in range(siblings)] + [grid_index]
    places = jnp.stack(places).astype(jnp.int32)

    blocks_here = local_rows // BLK
    pattern = lax.dynamic_slice(
        block_pattern, (child_front, grid_index * blocks_here), (1, blocks_here)
    )
    keep = jnp.repeat(pattern[0].astype(jnp.float32), BLK)
    lower_panel = lower_root * keep[:, None]
    root_rows = lax.all_gather(root_inverse, "leaf", axis=1, tiled=True)
    panels = [lower_panel[:, c * chunk : (c + 1) * chunk] for c in chunks]
    if square:
        middle_blocks, _ = gather_chips(middle_panel)
        first_blocks, _ = gather_chips(panels[0])
        near_by = [first_blocks[e] for e in (3, 5)]
    else:
        middle_blocks = doubled_hops(middle_panel)
        first_blocks, near_by = doubled_hops(panels[0]), []
    middle_blocks = gather_cores(middle_blocks)
    lower_blocks = [gather_cores(first_blocks)]
    panels[1:] = after(panels[1:], (middle_blocks, near_by))
    ready = after(root_rows, (panels[1:], lower_blocks))
    first_halves = [root_times(index, ready, middle_blocks, 0, 2)]
    ready = after(ready, first_halves)
    first_halves.append(root_times(index, ready, middle_blocks, 1, 2))
    arrived = [first_halves[1]]
    for panel in panels[1:]:
        if square:
            blocks, _ = gather_chips(panel, (lower_blocks, first_halves))
            arrived += [blocks[e] for e in (1, 2, 4)]
        else:
            blocks = doubled_hops(panel)
        lower_blocks.append(gather_cores(blocks))

    spots = []
    for e in range(grid_count):
        start = (grid_index ^ e) * middle_count
        spots += [(start // own_columns) ^ sibling_index, start % own_columns]
    spots = jnp.stack(spots).astype(jnp.int32)

    def transposed(parts):
        kept, other = pick(spots, parts, middle_count)
        outgoing = pair(kept, swap(other, "grid", 1), grid_count // 2)
        return outgoing, [outgoing[0]] + [
            swap(outgoing[k], "grid", 2 * k) for k in range(1, len(outgoing))
        ]

    sent = [
        [half] + [swap(half, "leaf", s) for s in range(1, siblings)] for half in first_halves
    ]
    global_rows = grid_index * middle_count + jnp.arange(middle_count, dtype=jnp.int32)
    global_columns = sibling_index * own_columns + jnp.arange(own_columns, dtype=jnp.int32)
    on_diagonal = global_rows[:, None] == global_columns[None, :]
    first_side = jnp.concatenate(first_halves, axis=0)
    middle_cross = -first_side
    middle_part = jnp.sum(jnp.where(on_diagonal, middle_inverse, 0.0), axis=0) + jnp.sum(
        middle_panel * first_side, axis=0
    )
    sent[0] = after(sent[0], (arrived, middle_cross, middle_part))
    outgoing, upper_columns = transposed(sent[0])
    ready = after(root_rows, outgoing)
    root_sides = [root_times(index, ready, lower_blocks[0])]
    sent[1] = after(sent[1], root_sides)
    outgoing, lower_columns = transposed(sent[1])
    left = [[sent[0][s], sent[1][s]] for s in range(siblings)]
    (mixed,) = mixed_times(places, after(left, outgoing), lower_middle)
    ready = after(root_rows, mixed)
    root_sides += [root_times(index, ready, blocks) for blocks in lower_blocks[1:]]
    root_side = jnp.concatenate(root_sides, axis=1) - mixed

    side_columns = [part for pair in zip(upper_columns, lower_columns) for part in pair]
    side_columns = after(side_columns, root_sides)
    shared = middle_inverse + side_times(side_columns, middle_blocks)
    shared_parts = [[shared]] + [[swap(shared, "leaf", s)] for s in range(1, siblings)]
    side_columns = after(side_columns, shared)
    side_products = [side_times(side_columns, blocks) for blocks in lower_blocks]
    shared_parts = after(shared_parts, side_products)
    lower_parent, parent_part = mixed_times(places, shared_parts, lower_middle, side_products)

    lower_part = jnp.sum(lower_panel * root_side, axis=0) + parent_part[0]

    total = jnp.concatenate([middle_part, lower_part])
    flip = 1
    while flip < grid_count:
        total = total + swap(total, "grid", flip)
        flip *= 2
    middle_total = total[:own_columns]
    lower_total = total[own_columns:]
    return (middle_cross, middle_total, -root_side, lower_parent, lower_diagonal + lower_total)


def solution(mesh):
    in_specs = (
        P("grid", "leaf"),
        P("grid", "leaf"),
        P("grid", "leaf"),
        P("grid", "leaf"),
        P(None, "leaf"),
        P(),
        P("leaf"),
    )
    out_specs = (P("grid", "leaf"), P("leaf"), P("grid", "leaf"), P("grid", "leaf"), P("leaf"))
    return jax.shard_map(local, mesh=mesh, in_specs=in_specs, out_specs=out_specs, check_vma=False)
```
